32 devices in a mesh: seq: 16 (over z, y, x), tensor: 2 (over core).
Axes of the slice: x: 2, y: 2, z: 4, core: 2. Of those that a mesh axis runs over, the one named last changes fastest.
Arguments:
- residual: bfloat16 [2048, 2048], P('seq', 'tensor'), may hold values from -10 to 10
- queries: bfloat16 [2048, 2048], P('seq', 'tensor'), may hold values from -5 to 5
- new_keys: bfloat16 [2048, 2048], P('seq', 'tensor'), may hold values from -5 to 5
- new_values: bfloat16 [2048, 2048], P('seq', 'tensor'), may hold values from -6 to 6
- cache_keys: bfloat16 [4, 8192, 2048], P(None, 'seq', 'tensor'), may hold values from -5 to 5
- cache_values: bfloat16 [4, 8192, 2048], P(None, 'seq', 'tensor'), may hold values from -6 to 6
- cache_lengths: int32 [4], replicated, may hold values from 1 to 8192, 9728 in all
- out_proj: bfloat16 [2048, 2048], P('tensor'), may hold values from -0.125 to 0.125
- norm_gain: float32 [2048], P('tensor'), may hold values from 0.5 to 1.5
- router: bfloat16 [2048, 32], P('tensor'), may hold values from -0.3984375 to 0.3984375
- expert_ids: int32 [2048, 6], P('seq'), may hold values from 0 to 31, all different within a row; in each aligned block of 128 rows (0 to 127, 128 to 255, ...) at most 32 rows name the same one
- expert_gate_up: bfloat16 [32, 2048, 2, 1408], P('seq', None, None, 'tensor'), may hold values from -0.125 to 0.125
- expert_down: bfloat16 [32, 1408, 2048], P('seq', 'tensor'), may hold values from -0.15625 to 0.15625
- shared_gate_up: bfloat16 [2048, 2, 1408], P(None, None, 'tensor'), may hold values from -0.125 to 0.125
- shared_down: bfloat16 [1408, 2048], P('tensor'), may hold values from -0.15625 to 0.15625
Outputs:
- layer_out: bfloat16 [2048, 2048], P('seq', 'tensor')
The draws below stay inside these ranges and needn't reach their ends.
Inputs may be any that keep to these rules, and one draw needn't show every extreme that they name: Request r's cached tokens are positions 0 to cache_lengths[r] - 1 of its row of 8192 cache positions; the lengths sum to 8192 + 3 * (512) and the longest equals 8192. `expert_ids`: each row names 6 different experts. Among the 128 rows of one index of seq no expert is named by more than 32 rows, and this bound is reached.
All inputs are finite; a program needn't handle non-finite values.
Results may differ from the reference program's by a relative error of at most 0.025.
Values may be sent and summed in bfloat16 or wider, within the bound.
A program may use at most 128 MiB of HBM per device.

```python
import math
import jax
import jax.numpy as jnp
import numpy as np
from jax import lax

D = 2048
HEADS = 16
HD = 128
FFE = 1408
SHF = 1408
TOPK = 6
NEW = 512
TOK_DEV = 128
CLEN_DEV = 512
TOKENS = 2048
REQS = 4
CLEN = 8192
EXPERTS = 32
CAP = 32
N_SEQ = 16
N_TENSOR = 2


def sign_table(key):
    flips = jax.random.bernoulli(jax.random.fold_in(key, 101), 0.5, (REQS, HEADS * HD))
    return jnp.where(flips, 1.0, -1.0).astype(jnp.float32)


def planted_levels():
    places = lax.iota(jnp.int32, NEW)
    levels = 3.5 + 0.5 * places.astype(jnp.float32)
    return jnp.where((places >= 1) & (places <= 3), levels, 0.0)


def draw_residual(key, part):
    columns = lax.iota(jnp.float32, D) / D
    spread = jnp.power(10.0, jax.random.uniform(jax.random.fold_in(key, 11), (D,), jnp.float32))
    noise = jnp.clip(jax.random.normal(jax.random.fold_in(key, 12), (TOKENS, D), jnp.float32), -4.0, 4.0)
    values = 0.02 * jnp.power(3.0, columns) * spread * noise
    return values.astype(jnp.bfloat16)


def draw_queries(key, part):
    width = HEADS * HD
    noise = jnp.clip(jax.random.normal(jax.random.fold_in(key, 21), (REQS, NEW, width), jnp.float32), -4.0, 4.0)
    levels = planted_levels()
    planted = levels[None, :, None] * sign_table(key)[:, None, :]
    values = jnp.where(levels[None, :, None] > 0.0, planted, noise)
    return values.reshape(TOKENS, width).astype(jnp.bfloat16)


def draw_cache_keys(key, part):
    width = HEADS * HD
    noise = jnp.clip(1.25 * jax.random.normal(jax.random.fold_in(key, 31), (REQS, CLEN, width), jnp.float32), -5.0, 5.0)
    first = (lax.iota(jnp.int32, CLEN) == 0)[None, :, None]
    values = jnp.where(first, 5.0 * sign_table(key)[:, None, :], noise)
    return values.astype(jnp.bfloat16)


def draw_new_keys(key, part):
    width = HEADS * HD
    noise = jnp.clip(1.25 * jax.random.normal(jax.random.fold_in(key, 41), (REQS, NEW, width), jnp.float32), -5.0, 5.0)
    first = (lax.iota(jnp.int32, NEW) == 0)[None, :, None]
    values = jnp.where(first, 4.9375 * sign_table(key)[:, None, :], noise)
    return values.reshape(TOKENS, width).astype(jnp.bfloat16)


def block_scale(rng, dims, cuts, smallest, largest):
    level, own = 1.0, jax.random.fold_in(rng, 6)
    for dim, shards_of in cuts:
        heights = jnp.exp(jax.random.uniform(jax.random.fold_in(own, dim), (shards_of,), jnp.float32, smallest / len(cuts), largest / len(cuts)))
        level = level * jnp.repeat(heights, dims[dim] // shards_of).reshape([-1 if axis == dim else 1 for axis in range(len(dims))])
    return level


def profile(number_of, total, most, slope):
    portions = [(1 << 20) // math.isqrt(standing ** slope) + 1 for standing in range(2, number_of + 1)]
    rest, holding = total - most - (number_of - 1), [1] * (number_of - 1)
    while rest > 0:
        candidates = [i for i in range(number_of - 1) if holding[i] < most]
        mass, remaining = sum([portions[i] for i in candidates]), rest
        for i in candidates:
            addition = min(most - holding[i], max(1, remaining * portions[i] // mass), rest)
            holding[i] = holding[i] + addition
            rest = rest - addition
    return np.array([most] + holding)


def uneven_parts(own_key, count, total, limit, lean):
    if count == 2:
        one = jax.random.randint(own_key, (), max(1, total - limit), min(limit, total - 1) + 1)
        return jnp.stack([one, total - one])
    sizes = jnp.asarray(profile(count, total, limit, lean), jnp.int32)
    couples = (count - 1) // 2
    source_of, taker = sizes[1:1 + 2 * couples:2], sizes[2:2 + 2 * couples:2]
    slack = jnp.minimum(source_of - 1, limit - taker)
    moved = jax.random.randint(jax.random.fold_in(own_key, 1), (couples,), 0, 1 << 20) % (slack + 1)
    sizes = sizes.at[1:1 + 2 * couples:2].set(source_of - moved).at[2:2 + 2 * couples:2].set(taker + moved)
    return sizes[jax.random.permutation(jax.random.fold_in(own_key, 2), count)]


def routed_block(key, own, number, rows, number_of, top, reach, slope):
    ranking = jax.random.permutation(key, number_of)
    packed, common = shares(number_of, rows * top, reach, slope, True), shares(number_of, rows * top, reach, slope, False)
    places = jnp.arange(number_of)

    def named(tallies, offset_by):
        used = int((tallies > 0).sum())
        fixed = max(1, used // 4)
        moved = fixed + (places - fixed + offset_by * (used - fixed)) % max(1, number_of - fixed)
        return jnp.zeros((number_of,), jnp.int32).at[ranking[jnp.where(places < fixed, places, moved)]].set(jnp.asarray(tallies, jnp.int32))

    tallies = jnp.where(number % 4 == 0, named(packed, number // 4), named(common, number - number // 4 - 1))
    mixed = jax.random.permutation(jax.random.fold_in(own, 3), number_of)
    source_of, receiver = mixed[0:number_of // 2 * 2:2], mixed[1:number_of // 2 * 2:2]
    margin = jnp.minimum(tallies[source_of] - 1, reach - tallies[receiver]) // 2
    margin = jnp.where((source_of == ranking[0]) | (receiver == ranking[0]) | (tallies[receiver] == 0), 0, jnp.maximum(margin, 0))
    moved = jax.random.randint(jax.random.fold_in(own, 4), (number_of // 2,), 0, 1 << 20) % (margin + 1)
    tallies = tallies.at[source_of].add(-moved).at[receiver].add(moved)
    labels = jnp.searchsorted(jnp.cumsum(tallies), jnp.arange(rows * top), side="right").astype(jnp.int32)
    grid = labels.reshape(top, rows).T
    grid = grid[jax.random.permutation(jax.random.fold_in(own, 1), rows)]
    offset_by = jax.random.randint(jax.random.fold_in(own, 2), (rows, 1), 0, top)
    return jnp.take_along_axis(grid, (jnp.arange(top)[None, :] + offset_by) % top, axis=1)


def shares(amount, total, bound, lean, full):
    weights = [(1 << 20) // math.isqrt(grade ** lean) + 1 for grade in range(1, amount + 1)]
    largest = bound if full else min(bound, max(-(-total // amount), total * weights[0] // sum(weights)))
    least = 1 if total - largest >= amount - 1 else 0
    holding, rest = [largest] + [least] * (amount - 1), total - largest - least * (amount - 1)
    while rest > 0:
        candidates = [i for i in range(1, amount) if holding[i] < largest] or [i for i in range(1, amount) if holding[i] < bound]
        pool, budget = sum([weights[i] for i in candidates]), rest
        for i in candidates:
            extra = min(bound - holding[i], max(1, budget * weights[i] // pool), rest)
            holding[i] = holding[i] + extra
            rest = rest - extra
    return np.array(holding)


def scatter_about(key, dims, scale, reach, pieces=(), kind=jnp.bfloat16):
    array = jax.random.normal(key, dims, jnp.float32) * scale
    if len(pieces) > 0:
        array = block_scale(key, dims, pieces, -0.22, 0.18) * array
    return jnp.clip(array, min=-reach, max=reach).astype(kind)


def setup_inputs(seed: int = 0) -> dict:
    streams_of = jax.random.split(jax.random.key(seed), 16)
    residual = draw_residual(jax.random.fold_in(streams_of[15], 71), 0)
    queries = draw_queries(jax.random.fold_in(streams_of[15], 71), 0)
    new_keys = draw_new_keys(jax.random.fold_in(streams_of[15], 71), 0)
    new_values = scatter_about(streams_of[3], (TOKENS, HEADS * HD), 1.0, 6.0, ((0, 16), (1, 2)))
    cache_keys = draw_cache_keys(jax.random.fold_in(streams_of[15], 71), 0)
    cache_values = scatter_about(streams_of[5], (REQS, CLEN, HEADS * HD), 1.0, 6.0, ((1, 16), (2, 2)))
    cache_lengths = uneven_parts(streams_of[6], REQS, CLEN + (REQS - 1) * (CLEN // 16), CLEN, 2).astype(jnp.int32)
    out_proj = scatter_about(streams_of[7], (HEADS * HD, D), (HEADS * HD) ** -0.5, 0.125, ((0, 2),))
    norm_gain = jnp.clip(1.0 + 0.1 * jax.random.normal(streams_of[8], (D,), jnp.float32), 0.5, 1.5)
    router = scatter_about(streams_of[9], (D, EXPERTS), 0.066, 0.3984375, ((0, 2),))
    expert_ids_keys = jax.random.split(jax.random.fold_in(streams_of[10], 1), TOKENS // TOK_DEV)
    expert_ids_turns = jax.random.permutation(jax.random.fold_in(streams_of[10], 3), TOKENS // TOK_DEV)
    expert_ids = jax.vmap(lambda own, number: routed_block(jax.random.fold_in(streams_of[10], 2), own, number, TOK_DEV, EXPERTS, TOPK, CAP, 2))(expert_ids_keys, expert_ids_turns).reshape((TOKENS, TOPK))
    expert_gate_up = scatter_about(streams_of[11], (EXPERTS, D, 2, FFE), D ** -0.5, 0.125, ((0, 16), (3, 2)))
    expert_down = scatter_about(streams_of[12], (EXPERTS, FFE, D), FFE ** -0.5, 0.15625, ((0, 16), (1, 2)))
    shared_gate_up = scatter_about(streams_of[13], (D, 2, SHF), D ** -0.5, 0.125, ((2, 2),))
    shared_down = scatter_about(streams_of[14], (SHF, D), SHF ** -0.5, 0.15625, ((0, 2),))
    return {"residual": residual, "queries": queries, "new_keys": new_keys, "new_values": new_values, "cache_keys": cache_keys, "cache_values": cache_values, "cache_lengths": cache_lengths, "out_proj": out_proj, "norm_gain": norm_gain, "router": router, "expert_ids": expert_ids, "expert_gate_up": expert_gate_up, "expert_down": expert_down, "shared_gate_up": shared_gate_up, "shared_down": shared_down}


negative = -1e+30
epsilon = 1e-06

def block_partial(scores, visible, values):
    masked = jnp.where(visible, scores, negative)
    block_max = lax.optimization_barrier(jnp.max(masked, -1))
    shifted = jnp.where(visible, scores, block_max[..., None]) - block_max[..., None]
    weights = jnp.where(visible, jnp.exp(shifted), 0.0)
    block_sum = lax.optimization_barrier(jnp.sum(weights, -1))
    rounded = lax.optimization_barrier(weights.astype(jnp.bfloat16)).astype(jnp.float32)
    block_out = jnp.einsum('hqbk,bkhd->hqbd', rounded, values.astype(jnp.float32))
    return (block_max, block_sum, block_out)

def one_request(request):
    query_rows, keys_cached, values_cached, keys_new, values_new, length = request
    scaling = 1.0 / math.sqrt(HD)
    queries_wide = query_rows.astype(jnp.float32)
    new_blocks = NEW // TOK_DEV
    cached_scores = jnp.einsum('qhd,khd->hqk', queries_wide, keys_cached.astype(jnp.float32)) * scaling
    cached_scores = cached_scores.reshape(HEADS, NEW, N_SEQ, CLEN_DEV)
    visible_cached = (lax.iota(jnp.int32, CLEN) < length.astype(jnp.int32)).reshape(1, 1, N_SEQ, CLEN_DEV)
    max_cached, sum_cached, out_cached = block_partial(cached_scores, visible_cached, values_cached.reshape(N_SEQ, CLEN_DEV, HEADS, HD))
    new_scores = jnp.einsum('qhd,khd->hqk', queries_wide, keys_new.astype(jnp.float32)) * scaling
    new_scores = new_scores.reshape(HEADS, NEW, new_blocks, TOK_DEV)
    places = lax.iota(jnp.int32, NEW)
    visible_new = (places[:, None] >= places[None, :]).reshape(1, NEW, new_blocks, TOK_DEV)
    max_new, sum_new, out_new = block_partial(new_scores, visible_new, values_new.reshape(new_blocks, TOK_DEV, HEADS, HD))
    block_max = jnp.concatenate([max_cached, max_new], -1)
    block_sum = jnp.concatenate([sum_cached, sum_new], -1)
    block_out = jnp.concatenate([out_cached, out_new], 2)
    row_max = lax.optimization_barrier(jnp.max(block_max, -1))
    factors = jnp.exp(block_max - row_max[..., None])
    row_sum = lax.optimization_barrier(jnp.sum(block_sum * factors, -1))
    weighted = lax.optimization_barrier(jnp.sum(block_out * factors[..., None], 2))
    attended = (weighted / row_sum[..., None]).astype(jnp.bfloat16)
    return jnp.transpose(attended, (1, 0, 2)).reshape(NEW, HEADS * HD)

def routed_outputs(normed, expert_ids, expert_gate_up, expert_down):
    flat_ids = expert_ids.reshape(-1).astype(jnp.int32)
    count = flat_ids.shape[0]
    padded = jnp.concatenate([normed, jnp.zeros((1, D), normed.dtype)], 0)
    most_rows = N_SEQ * CAP
    group = FFE // N_TENSOR

    def one_expert(expert, result):
        places = jnp.nonzero(flat_ids == expert, size=most_rows, fill_value=count)[0].astype(jnp.int32)
        rows = padded[(places // TOPK).astype(jnp.int32)].astype(jnp.float32)
        gate_up = expert_gate_up[expert].astype(jnp.float32).reshape(D, 2, N_TENSOR, group)
        pair = jnp.einsum('md,dcjg->mcjg', rows, gate_up)
        hidden_act = (jax.nn.silu(pair[:, 0]) * pair[:, 1]).astype(jnp.bfloat16)
        down = expert_down[expert].astype(jnp.float32).reshape(N_TENSOR, group, D)
        parts = jnp.einsum('mjg,jgd->mjd', hidden_act.astype(jnp.float32), down).astype(jnp.bfloat16)
        outputs = lax.optimization_barrier(jnp.sum(parts.astype(jnp.float32), 1)).astype(jnp.bfloat16)
        return result.at[places].set(outputs, mode='drop')
    result = lax.fori_loop(0, EXPERTS, one_expert, jnp.zeros((count, D), jnp.bfloat16))
    return result.reshape(TOKENS, TOPK, D)

def reference(residual, queries, new_keys, new_values, cache_keys, cache_values, cache_lengths, out_proj, norm_gain, router, expert_ids, expert_gate_up, expert_down, shared_gate_up, shared_down):
    requests = (queries.reshape(REQS, NEW, HEADS, HD), cache_keys.reshape(REQS, CLEN, HEADS, HD), cache_values.reshape(REQS, CLEN, HEADS, HD), new_keys.reshape(REQS, NEW, HEADS, HD), new_values.reshape(REQS, NEW, HEADS, HD), cache_lengths.astype(jnp.int32))
    attended = lax.map(one_request, requests).reshape(TOKENS, HEADS * HD)
    attn_out = jnp.dot(attended, out_proj, preferred_element_type=jnp.float32)
    stream = residual.astype(jnp.float32) + attn_out
    inverse_rms = lax.rsqrt(lax.optimization_barrier(jnp.mean(stream * stream, 1)) + epsilon)
    normed = (stream * inverse_rms[:, None] * norm_gain).astype(jnp.bfloat16)
    logits = jnp.dot(normed, router, preferred_element_type=jnp.float32)
    chosen = jax.nn.sigmoid(jnp.take_along_axis(logits, expert_ids.astype(jnp.int32), 1))
    gates = chosen / lax.optimization_barrier(jnp.sum(chosen, 1, keepdims=True))
    pair = jnp.einsum('td,dcf->tcf', normed.astype(jnp.float32), shared_gate_up.astype(jnp.float32))
    shared_act = (jax.nn.silu(pair[:, 0]) * pair[:, 1]).astype(jnp.bfloat16)
    shared_out = jnp.dot(shared_act, shared_down, preferred_element_type=jnp.float32)
    routed = routed_outputs(normed, expert_ids, expert_gate_up, expert_down)
    mixture = lax.optimization_barrier(jnp.sum(gates[..., None] * routed.astype(jnp.float32), 1))
    return (stream + shared_out + mixture).astype(jnp.bfloat16)
```

```python
import math

import jax
import jax.numpy as jnp
from jax import lax
from jax.experimental import pallas as pl
from jax.experimental.pallas import tpu as pltpu
from jax.sharding import PartitionSpec as P

D = 2048
HD = 128
NEW = 512


negative = -1e30
epsilon = 1e-06


LOG2E = 1.4426950408889634
STAT_ROWS = 16


def attention_kernel(
    tok_dev, len_ref, q_ref, k_ref, v_ref, nk_ref, nv_ref, out_ref
):
    request = pl.program_id(0)
    seq_index = lax.axis_index("seq")
    own_start = seq_index * tok_dev
    clen_dev = k_ref.shape[1]
    rows = q_ref.shape[0]
    quarters = rows // tok_dev
    own = own_start // rows == request
    remaining = len_ref[request] - seq_index * clen_dev
    scale = LOG2E / math.sqrt(HD)

    def scored(keys):
        return (
            lax.dot_general(
                keys, q_ref[...], (((1,), (1,)), ((), ())), preferred_element_type=jnp.float32
            )
            * scale
        )

    def weighted(weights, values):
        return lax.dot_general(
            weights.astype(jnp.bfloat16),
            values,
            (((0,), (0,)), ((), ())),
            preferred_element_type=jnp.float32,
        )

    def emit(out, top, total):
        high = total.astype(jnp.bfloat16).astype(jnp.float32)
        row = lax.broadcasted_iota(jnp.int32, (STAT_ROWS, rows), 0)
        stats = jnp.where(
            row == 0, top, jnp.where(row == 1, high, jnp.where(row == 2, total - high, 0.0))
        ).astype(jnp.bfloat16)
        for part in range(quarters):
            window = slice(part * tok_dev, (part + 1) * tok_dev)
            out_ref[part, :tok_dev, :] = out[window].astype(jnp.bfloat16)
            out_ref[part, tok_dev:, :] = stats[:, window]

    def rounded(top):
        return top.astype(jnp.bfloat16).astype(jnp.float32)

    visible = lax.broadcasted_iota(jnp.int32, (clen_dev, rows), 0) < remaining

    @pl.when(own)
    def _():
        cached = jnp.where(visible, scored(k_ref[0]), negative)
        place = lax.broadcasted_iota(jnp.int32, (tok_dev, rows), 0) + own_start % rows
        seen = place <= lax.broadcasted_iota(jnp.int32, (tok_dev, rows), 1)
        fresh = jnp.where(seen, scored(nk_ref[...]), negative)
        top = rounded(
            jnp.maximum(jnp.max(cached, 0, keepdims=True), jnp.max(fresh, 0, keepdims=True))
        )
        cached = jnp.where(visible, jnp.exp2(cached - top), 0.0)
        fresh = jnp.where(seen, jnp.exp2(fresh - top), 0.0)
        total = jnp.sum(cached, 0, keepdims=True) + jnp.sum(fresh, 0, keepdims=True)
        emit(weighted(cached, v_ref[0]) + weighted(fresh, nv_ref[...]), top, total)

    @pl.when(jnp.logical_not(own) & (remaining > 0))
    def _():
        cached = jnp.where(visible, scored(k_ref[0]), negative)
        top = rounded(jnp.max(cached, 0, keepdims=True))
        cached = jnp.where(visible, jnp.exp2(cached - top), 0.0)
        emit(weighted(cached, v_ref[0]), top, jnp.sum(cached, 0, keepdims=True))

    @pl.when(jnp.logical_not(own) & (remaining <= 0))
    def _():
        emit(
            jnp.zeros((rows, HD), jnp.float32),
            jnp.full((1, rows), negative, jnp.float32),
            jnp.zeros((1, rows), jnp.float32),
        )


def attention(lengths, every_query, cache_keys, cache_values, new_keys, new_values):
    requests, clen_dev, width = cache_keys.shape
    tok_dev = new_keys.shape[0]
    tokens = every_query.shape[0]
    heads = width // HD
    quarters = NEW // tok_dev
    return pl.pallas_call(
        lambda *refs: attention_kernel(tok_dev, *refs),
        grid_spec=pltpu.PrefetchScalarGridSpec(
            num_scalar_prefetch=1,
            grid=(requests, heads),
            in_specs=[
                pl.BlockSpec((NEW, HD), lambda r, h, n: (r, h)),
                pl.BlockSpec((1, clen_dev, HD), lambda r, h, n: (r, 0, h)),
                pl.BlockSpec((1, clen_dev, HD), lambda r, h, n: (r, 0, h)),
                pl.BlockSpec((tok_dev, HD), lambda r, h, n: (0, h)),
                pl.BlockSpec((tok_dev, HD), lambda r, h, n: (0, h)),
            ],
            out_specs=pl.BlockSpec(
                (quarters, tok_dev + STAT_ROWS, HD), lambda r, h, n: (r, 0, h)
            ),
        ),
        out_shape=jax.ShapeDtypeStruct(
            (tokens // tok_dev, tok_dev + STAT_ROWS, width), jnp.bfloat16
        ),
        compiler_params=pltpu.CompilerParams(vmem_limit_bytes=32 * 1024 * 1024),
        cost_estimate=pl.CostEstimate(
            flops=4 * NEW * clen_dev * width * 2,
            bytes_accessed=16 * 1024 * 1024,
            transcendentals=2 * NEW * clen_dev * heads,
        ),
        name="ragged_attention",
    )(lengths, every_query, cache_keys, cache_values, new_keys, new_values)


def combine_kernel(parts_ref, out_ref):
    sources = parts_ref.shape[0]
    tok_dev = out_ref.shape[0]
    stats = [
        parts_ref[source, tok_dev:, :].astype(jnp.float32) for source in range(sources)
    ]
    tops = jnp.concatenate([stat[0:1] for stat in stats], 0)
    sums = jnp.concatenate([stat[1:2] + stat[2:3] for stat in stats], 0)
    factors = jnp.exp2(tops - jnp.max(tops, 0, keepdims=True))
    factors = factors / jnp.sum(factors * sums, 0, keepdims=True)
    columns = factors.T
    total = jnp.zeros((tok_dev, HD), jnp.float32)
    for source in range(sources):
        total += columns[:, source : source + 1] * parts_ref[source, :tok_dev, :].astype(
            jnp.float32
        )
    out_ref[...] = total.astype(jnp.bfloat16)


def combine(parts):
    sources, rows, width = parts.shape
    tok_dev = rows - STAT_ROWS
    return pl.pallas_call(
        combine_kernel,
        grid=(width // HD,),
        in_specs=[pl.BlockSpec((sources, rows, HD), lambda h: (0, 0, h))],
        out_specs=pl.BlockSpec((tok_dev, HD), lambda h: (0, h)),
        out_shape=jax.ShapeDtypeStruct((tok_dev, width), jnp.bfloat16),
        compiler_params=pltpu.CompilerParams(vmem_limit_bytes=32 * 1024 * 1024),
        name="combine_blocks",
    )(parts)


def shards(
    residual,
    queries,
    new_keys,
    new_values,
    cache_keys,
    cache_values,
    cache_lengths,
    out_proj,
    norm_gain,
    router,
    expert_ids,
    expert_gate_up,
    expert_down,
    shared_gate_up,
    shared_down,
):
    seq_count = lax.axis_size("seq")
    tensor_count = lax.axis_size("tensor")
    tok_dev = queries.shape[0]
    width_local = residual.shape[1]
    experts = router.shape[1]
    exp_dev = expert_gate_up.shape[0]
    topk = expert_ids.shape[1]
    every_query = lax.all_gather(queries, "seq", axis=0, tiled=True)
    partials = attention(
        cache_lengths, every_query, cache_keys, cache_values, new_keys, new_values
    )
    attended = combine(
        lax.all_to_all(partials, "seq", split_axis=0, concat_axis=0, tiled=True)
    )
    projected = jnp.dot(attended, out_proj, preferred_element_type=jnp.float32)
    attn_out = lax.psum_scatter(
        projected.astype(jnp.bfloat16), "tensor", scatter_dimension=1, tiled=True
    ).astype(jnp.float32)
    stream = residual.astype(jnp.float32) + attn_out
    square_total = lax.psum(jnp.sum(stream * stream, 1), "tensor")
    inverse_rms = lax.rsqrt(square_total / D + epsilon)
    normed = (stream * inverse_rms[:, None] * norm_gain).astype(jnp.bfloat16)
    logits = lax.psum(
        jnp.dot(normed, router, preferred_element_type=jnp.float32).astype(jnp.bfloat16), "tensor"
    ).astype(jnp.float32)
    matches = expert_ids[:, :, None] == lax.iota(jnp.int32, experts)[None, None, :]
    selected = jnp.sum(jnp.where(matches, logits[:, None, :], 0.0), 2)
    sigmoids = jax.nn.sigmoid(selected)
    gates = sigmoids / jnp.sum(sigmoids, 1, keepdims=True)
    normed_full = lax.all_gather(normed, "tensor", axis=1, tiled=True)
    shared_pair = jnp.einsum(
        "td,dcf->tcf", normed_full, shared_gate_up, preferred_element_type=jnp.float32
    )
    shared_act = (jax.nn.silu(shared_pair[:, 0]) * shared_pair[:, 1]).astype(jnp.bfloat16)
    shared_term = jnp.dot(shared_act, shared_down, preferred_element_type=jnp.float32)
    shared_out = lax.psum_scatter(
        shared_term.astype(jnp.bfloat16), "tensor", scatter_dimension=1, tiled=True
    ).astype(jnp.float32)
    cap = tensor_count * (
        (4 * tok_dev * topk + 3 * experts * tensor_count - 1) // (3 * experts * tensor_count)
    )
    flat_ids = expert_ids.reshape(-1)
    marks = (flat_ids[:, None] == lax.iota(jnp.int32, experts)[None, :]).astype(jnp.int32)
    earlier = jnp.cumsum(marks, 0) - marks
    rank = jnp.sum(earlier * marks, 1)
    slot_index = flat_ids * cap + rank
    source_rows = (
        jnp.full((experts * cap,), tok_dev, jnp.int32)
        .at[slot_index]
        .set(lax.iota(jnp.int32, flat_ids.shape[0]) // topk)
    )
    padded_local = jnp.concatenate([normed, jnp.zeros((1, width_local), jnp.bfloat16)], 0)
    outgoing = padded_local[source_rows].reshape(seq_count, exp_dev, cap, width_local)
    incoming = lax.all_to_all(outgoing, "seq", split_axis=0, concat_axis=0, tiled=True)
    routed_rows = lax.all_gather(incoming, "tensor", axis=3, tiled=True)
    expert_pair = jnp.einsum(
        "secd,edjf->secjf", routed_rows, expert_gate_up, preferred_element_type=jnp.float32
    )
    expert_act = (jax.nn.silu(expert_pair[..., 0, :]) * expert_pair[..., 1, :]).astype(jnp.bfloat16)
    expert_term = jnp.einsum(
        "secf,efd->secd", expert_act, expert_down, preferred_element_type=jnp.float32
    )
    expert_total = lax.psum_scatter(
        expert_term.astype(jnp.bfloat16), "tensor", scatter_dimension=3, tiled=True
    )
    returned = lax.all_to_all(expert_total, "seq", split_axis=0, concat_axis=0, tiled=True)
    picked = returned.reshape(experts * cap, width_local)[slot_index].reshape(
        tok_dev, topk, width_local
    )
    mixture = jnp.sum(gates[..., None] * picked.astype(jnp.float32), 1)
    return (stream + shared_out + mixture).astype(jnp.bfloat16)


def solution(mesh):
    in_specs = (
        P("seq", "tensor"),
        P("seq", "tensor"),
        P("seq", "tensor"),
        P("seq", "tensor"),
        P(None, "seq", "tensor"),
        P(None, "seq", "tensor"),
        P(),
        P("tensor", None),
        P("tensor"),
        P("tensor", None),
        P("seq", None),
        P("seq", None, None, "tensor"),
        P("seq", "tensor", None),
        P(None, None, "tensor"),
        P("tensor", None),
    )
    out_specs = P("seq", "tensor")
    return jax.shard_map(shards, mesh=mesh, in_specs=in_specs, out_specs=out_specs, check_vma=False)
```

```python
import math

import jax
import jax.numpy as jnp
from jax import lax
from jax.experimental import pallas as pl
from jax.experimental.pallas import tpu as pltpu
from jax.sharding import PartitionSpec as P

D = 2048
HD = 128
NEW = 512


negative = -1e30
epsilon = 1e-06


LOG2E = 1.4426950408889634
STAT_ROWS = 16


def attention_kernel(
    tok_dev, len_ref, q_ref, k_ref, v_ref, nk_ref, nv_ref, out_ref
):
    request = pl.program_id(0)
    seq_index = lax.axis_index("seq")
    own_start = seq_index * tok_dev
    clen_dev = k_ref.shape[1]
    rows = q_ref.shape[0]
    quarters = rows // tok_dev
    own = own_start // rows == request
    remaining = len_ref[request] - seq_index * clen_dev
    scale = LOG2E / math.sqrt(HD)

    def scored(keys):
        return (
            lax.dot_general(
                keys, q_ref[...], (((1,), (1,)), ((), ())), preferred_element_type=jnp.float32
            )
            * scale
        )

    def weighted(weights, values):
        return lax.dot_general(
            weights.astype(jnp.bfloat16),
            values,
            (((0,), (0,)), ((), ())),
            preferred_element_type=jnp.float32,
        )

    def emit(out, top, total):
        high = total.astype(jnp.bfloat16).astype(jnp.float32)
        row = lax.broadcasted_iota(jnp.int32, (STAT_ROWS, rows), 0)
        stats = jnp.where(
            row == 0, top, jnp.where(row == 1, high, jnp.where(row == 2, total - high, 0.0))
        ).astype(jnp.bfloat16)
        for part in range(quarters):
            window = slice(part * tok_dev, (part + 1) * tok_dev)
            out_ref[part, :tok_dev, :] = out[window].astype(jnp.bfloat16)
            out_ref[part, tok_dev:, :] = stats[:, window]

    def rounded(top):
        return top.astype(jnp.bfloat16).astype(jnp.float32)

    visible = lax.broadcasted_iota(jnp.int32, (clen_dev, rows), 0) < remaining

    @pl.when(own)
    def _():
        cached = jnp.where(visible, scored(k_ref[0]), negative)
        place = lax.broadcasted_iota(jnp.int32, (tok_dev, rows), 0) + own_start % rows
        seen = place <= lax.broadcasted_iota(jnp.int32, (tok_dev, rows), 1)
        fresh = jnp.where(seen, scored(nk_ref[...]), negative)
        top = rounded(
            jnp.maximum(jnp.max(cached, 0, keepdims=True), jnp.max(fresh, 0, keepdims=True))
        )
        cached = jnp.where(visible, jnp.exp2(cached - top), 0.0)
        fresh = jnp.where(seen, jnp.exp2(fresh - top), 0.0)
        total = jnp.sum(cached, 0, keepdims=True) + jnp.sum(fresh, 0, keepdims=True)
        emit(weighted(cached, v_ref[0]) + weighted(fresh, nv_ref[...]), top, total)

    @pl.when(jnp.logical_not(own) & (remaining > 0))
    def _():
        cached = jnp.where(visible, scored(k_ref[0]), negative)
        top = rounded(jnp.max(cached, 0, keepdims=True))
        cached = jnp.where(visible, jnp.exp2(cached - top), 0.0)
        emit(weighted(cached, v_ref[0]), top, jnp.sum(cached, 0, keepdims=True))

    @pl.when(jnp.logical_not(own) & (remaining <= 0))
    def _():
        emit(
            jnp.zeros((rows, HD), jnp.float32),
            jnp.full((1, rows), negative, jnp.float32),
            jnp.zeros((1, rows), jnp.float32),
        )


def attention(first, heads, lengths, every_query, cache_keys, cache_values, new_keys, new_values):
    requests, clen_dev, width = cache_keys.shape
    tok_dev = new_keys.shape[0]
    tokens = every_query.shape[0]
    quarters = NEW // tok_dev
    return pl.pallas_call(
        lambda *refs: attention_kernel(tok_dev, *refs),
        grid_spec=pltpu.PrefetchScalarGridSpec(
            num_scalar_prefetch=1,
            grid=(requests, heads),
            in_specs=[
                pl.BlockSpec((NEW, HD), lambda r, h, n: (r, first + h)),
                pl.BlockSpec((1, clen_dev, HD), lambda r, h, n: (r, 0, first + h)),
                pl.BlockSpec((1, clen_dev, HD), lambda r, h, n: (r, 0, first + h)),
                pl.BlockSpec((tok_dev, HD), lambda r, h, n: (0, first + h)),
                pl.BlockSpec((tok_dev, HD), lambda r, h, n: (0, first + h)),
            ],
            out_specs=pl.BlockSpec(
                (quarters, tok_dev + STAT_ROWS, HD), lambda r, h, n: (r, 0, h)
            ),
        ),
        out_shape=jax.ShapeDtypeStruct(
            (tokens // tok_dev, tok_dev + STAT_ROWS, heads * HD), jnp.bfloat16
        ),
        compiler_params=pltpu.CompilerParams(vmem_limit_bytes=32 * 1024 * 1024),
        cost_estimate=pl.CostEstimate(
            flops=4 * requests * NEW * clen_dev * heads * HD * 4,
            bytes_accessed=16 * 1024 * 1024,
            transcendentals=2 * NEW * clen_dev * heads,
        ),
        name="ragged_attention",
    )(lengths, every_query, cache_keys, cache_values, new_keys, new_values)


def gather_kernel(
    own_ref, out_ref, local_sem, zs, zr, xs, xr, ys, yr, fs, fr, gs, gr
):
    rows = own_ref.shape[0]
    half = rows // 2
    planes = lax.axis_size("seq") // 4
    me = lax.axis_index("seq")
    plane, corner = me // 4, me % 4
    side_x = corner + 1 - 2 * (corner % 2)
    side_y = (corner + 2) % 4
    step_by = jnp.where(plane < planes // 2, 1, planes - 1)

    def plane_at(k):
        return (plane + k * step_by) % planes

    def rows_of(index, start=0, size=rows):
        return pl.ds(pl.multiple_of(index * rows + start, half), size)

    def copy(src, dst, send, recv, target):
        return pltpu.make_async_remote_copy(
            src_ref=src,
            dst_ref=dst,
            send_sem=send,
            recv_sem=recv,
            device_id={"seq": target},
            device_id_type=pl.DeviceIdType.MESH,
        )

    barrier = pltpu.get_barrier_semaphore()
    peers = [plane_at(k) * 4 + corner for k in range(1, planes)]
    peers += [plane * 4 + side_x, plane * 4 + side_y]
    for peer in peers:
        pl.semaphore_signal(
            barrier, inc=1, device_id={"seq": peer}, device_id_type=pl.DeviceIdType.MESH
        )
    pl.semaphore_wait(barrier, len(peers))

    mine = pltpu.make_async_copy(own_ref, out_ref.at[rows_of(me)], local_sem)
    mine.start()
    sends = []
    for k in range(1, planes):
        target = plane_at(k)
        send = copy(
            own_ref, out_ref.at[rows_of(me)], zs.at[k], zr.at[plane], target * 4 + corner
        )
        send.start()
        sends.append(send)

    def arrived(index, start, size, sem):
        place = out_ref.at[rows_of(index, start, size)]
        pltpu.make_async_copy(place, place, sem).wait()

    def forward(k):
        level = plane_at(k)
        from_y = level * 4 + side_y
        arrived(from_y, 0, rows, yr.at[k])
        place = out_ref.at[rows_of(from_y, 0, half)]
        send = copy(place, place, fs.at[k], fr.at[k], plane * 4 + side_x)
        send.start()
        sends.append(send)
        from_x = level * 4 + side_x
        arrived(from_x, 0, rows, xr.at[k])
        place = out_ref.at[rows_of(from_x, half, half)]
        send = copy(place, place, gs.at[k], gr.at[k], plane * 4 + side_y)
        send.start()
        sends.append(send)

    for k in range(planes):
        level = plane_at(k)
        index = level * 4 + corner
        if k > 0:
            arrived(index, 0, rows, zr.at[level])
        place = out_ref.at[rows_of(index)]
        source = own_ref if k == 0 else place
        for send in (
            copy(source, place, xs.at[k], xr.at[k], plane * 4 + side_x),
            copy(source, place, ys.at[k], yr.at[k], plane * 4 + side_y),
        ):
            send.start()
            sends.append(send)
        if k > 0:
            forward(k - 1)
    forward(planes - 1)
    diagonal = 3 - corner
    for k in range(planes):
        arrived(plane_at(k) * 4 + diagonal, 0, half, fr.at[k])
        arrived(plane_at(k) * 4 + diagonal, half, half, gr.at[k])
    for send in sends:
        send.wait_send()
    mine.wait()


def gather_rows(rows, count):
    planes = count // 4
    return pl.pallas_call(
        gather_kernel,
        in_specs=[pl.BlockSpec(memory_space=pl.ANY)],
        out_specs=pl.BlockSpec(memory_space=pl.ANY),
        out_shape=jax.ShapeDtypeStruct((rows.shape[0] * count, rows.shape[1]), rows.dtype),
        scratch_shapes=[pltpu.SemaphoreType.DMA] + [pltpu.SemaphoreType.DMA((planes,))] * 10,
        compiler_params=pltpu.CompilerParams(collective_id=0, has_side_effects=True),
        name="gather_rows",
    )(rows)


def combine_kernel(parts_ref, out_ref):
    sources = parts_ref.shape[0]
    tok_dev = out_ref.shape[0]
    stats = [
        parts_ref[source, tok_dev:, :].astype(jnp.float32) for source in range(sources)
    ]
    tops = jnp.concatenate([stat[0:1] for stat in stats], 0)
    sums = jnp.concatenate([stat[1:2] + stat[2:3] for stat in stats], 0)
    factors = jnp.exp2(tops - jnp.max(tops, 0, keepdims=True))
    factors = factors / jnp.sum(factors * sums, 0, keepdims=True)
    columns = factors.T
    total = jnp.zeros((tok_dev, HD), jnp.float32)
    for source in range(sources):
        total += columns[:, source : source + 1] * parts_ref[source, :tok_dev, :].astype(
            jnp.float32
        )
    out_ref[...] = total.astype(jnp.bfloat16)


def combine(parts):
    sources, rows, width = parts.shape
    tok_dev = rows - STAT_ROWS
    return pl.pallas_call(
        combine_kernel,
        grid=(width // HD,),
        in_specs=[pl.BlockSpec((sources, rows, HD), lambda h: (0, 0, h))],
        out_specs=pl.BlockSpec((tok_dev, HD), lambda h: (0, h)),
        out_shape=jax.ShapeDtypeStruct((tok_dev, width), jnp.bfloat16),
        compiler_params=pltpu.CompilerParams(vmem_limit_bytes=32 * 1024 * 1024),
        name="combine_blocks",
    )(parts)


def shards(
    residual,
    queries,
    new_keys,
    new_values,
    cache_keys,
    cache_values,
    cache_lengths,
    out_proj,
    norm_gain,
    router,
    expert_ids,
    expert_gate_up,
    expert_down,
    shared_gate_up,
    shared_down,
):
    seq_count = lax.axis_size("seq")
    tensor_count = lax.axis_size("tensor")
    tok_dev = queries.shape[0]
    width_local = residual.shape[1]
    experts = router.shape[1]
    exp_dev = expert_gate_up.shape[0]
    topk = expert_ids.shape[1]
    every_query = gather_rows(queries, seq_count)
    heads_local = queries.shape[1] // HD
    pieces = 2 if heads_local % 2 == 0 else 1
    heads_piece = heads_local // pieces
    projected = 0.0
    for piece in range(pieces):
        partials = attention(
            piece * heads_piece,
            heads_piece,
            cache_lengths,
            every_query,
            cache_keys,
            cache_values,
            new_keys,
            new_values,
        )
        attended = combine(
            lax.all_to_all(partials, "seq", split_axis=0, concat_axis=0, tiled=True)
        )
        features = slice(piece * heads_piece * HD, (piece + 1) * heads_piece * HD)
        projected += jnp.dot(
            attended, out_proj[features], preferred_element_type=jnp.float32
        )
    attn_out = lax.psum_scatter(
        projected.astype(jnp.bfloat16), "tensor", scatter_dimension=1, tiled=True
    ).astype(jnp.float32)
    stream = residual.astype(jnp.float32) + attn_out
    square_total = lax.psum(jnp.sum(stream * stream, 1), "tensor")
    inverse_rms = lax.rsqrt(square_total / D + epsilon)
    normed = (stream * inverse_rms[:, None] * norm_gain).astype(jnp.bfloat16)
    logits = lax.psum(
        jnp.dot(normed, router, preferred_element_type=jnp.float32).astype(jnp.bfloat16), "tensor"
    ).astype(jnp.float32)
    matches = expert_ids[:, :, None] == lax.iota(jnp.int32, experts)[None, None, :]
    selected = jnp.sum(jnp.where(matches, logits[:, None, :], 0.0), 2)
    sigmoids = jax.nn.sigmoid(selected)
    gates = sigmoids / jnp.sum(sigmoids, 1, keepdims=True)
    normed_full = lax.all_gather(normed, "tensor", axis=1, tiled=True)
    shared_pair = jnp.einsum(
        "td,dcf->tcf", normed_full, shared_gate_up, preferred_element_type=jnp.float32
    )
    shared_act = (jax.nn.silu(shared_pair[:, 0]) * shared_pair[:, 1]).astype(jnp.bfloat16)
    shared_term = jnp.dot(shared_act, shared_down, preferred_element_type=jnp.float32)
    shared_out = lax.psum_scatter(
        shared_term.astype(jnp.bfloat16), "tensor", scatter_dimension=1, tiled=True
    ).astype(jnp.float32)
    cap = tensor_count * (
        (4 * tok_dev * topk + 3 * experts * tensor_count - 1) // (3 * experts * tensor_count)
    )
    flat_ids = expert_ids.reshape(-1)
    marks = (flat_ids[:, None] == lax.iota(jnp.int32, experts)[None, :]).astype(jnp.int32)
    earlier = jnp.cumsum(marks, 0) - marks
    rank = jnp.sum(earlier * marks, 1)
    slot_index = flat_ids * cap + rank
    slots = (
        (slot_index // (exp_dev * cap)) * cap + slot_index % cap
    ).reshape(tok_dev, topk)
    member = (expert_ids % exp_dev).reshape(tok_dev, topk)
    mixture = 0.0
    for local in range(exp_dev):
        here = (slots[:, :, None] == lax.iota(jnp.int32, seq_count * cap)[None, None, :]) & (
            member[:, :, None] == local
        )
        placement = jnp.any(here, 1).astype(jnp.bfloat16)
        outgoing = lax.dot_general(
            placement, normed, (((0,), (0,)), ((), ())), preferred_element_type=jnp.float32
        ).astype(jnp.bfloat16)
        incoming = lax.all_to_all(
            outgoing.reshape(seq_count, cap, width_local),
            "seq",
            split_axis=0,
            concat_axis=0,
            tiled=True,
        ).reshape(seq_count * cap, width_local)
        routed_rows = lax.all_gather(incoming, "tensor", axis=1, tiled=True)
        expert_pair = jnp.einsum(
            "rd,djf->rjf",
            routed_rows,
            expert_gate_up[local],
            preferred_element_type=jnp.float32,
        )
        expert_act = (jax.nn.silu(expert_pair[:, 0]) * expert_pair[:, 1]).astype(jnp.bfloat16)
        expert_term = jnp.dot(
            expert_act, expert_down[local], preferred_element_type=jnp.float32
        )
        expert_total = lax.psum_scatter(
            expert_term.astype(jnp.bfloat16), "tensor", scatter_dimension=1, tiled=True
        )
        returned = lax.all_to_all(
            expert_total.reshape(seq_count, cap, width_local),
            "seq",
            split_axis=0,
            concat_axis=0,
            tiled=True,
        ).reshape(seq_count * cap, width_local)
        portions = jnp.sum(jnp.where(here, gates[:, :, None], 0.0), 1)
        high = portions.astype(jnp.bfloat16)
        low = (portions - high.astype(jnp.float32)).astype(jnp.bfloat16)
        mixture += jnp.dot(high, returned, preferred_element_type=jnp.float32) + jnp.dot(
            low, returned, preferred_element_type=jnp.float32
        )
    return (stream + shared_out + mixture).astype(jnp.bfloat16)


def solution(mesh):
    in_specs = (
        P("seq", "tensor"),
        P("seq", "tensor"),
        P("seq", "tensor"),
        P("seq", "tensor"),
        P(None, "seq", "tensor"),
        P(None, "seq", "tensor"),
        P(),
        P("tensor", None),
        P("tensor"),
        P("tensor", None),
        P("seq", None),
        P("seq", None, None, "tensor"),
        P("seq", "tensor", None),
        P(None, None, "tensor"),
        P("tensor", None),
    )
    out_specs = P("seq", "tensor")
    return jax.shard_map(shards, mesh=mesh, in_specs=in_specs, out_specs=out_specs, check_vma=False)
```

```python
import math

import jax
import jax.numpy as jnp
from jax import lax
from jax.experimental import pallas as pl
from jax.experimental.pallas import tpu as pltpu
from jax.sharding import PartitionSpec as P

D = 2048
HD = 128
NEW = 512


negative = -1e30
epsilon = 1e-06


LOG2E = 1.4426950408889634
STAT_ROWS = 16


def attention_kernel(
    tok_dev, len_ref, q_ref, k_ref, v_ref, nk_ref, nv_ref, out_ref
):
    request = pl.program_id(0)
    seq_index = lax.axis_index("seq")
    own_start = seq_index * tok_dev
    clen_dev = k_ref.shape[1]
    rows = q_ref.shape[0]
    quarters = rows // tok_dev
    own = own_start // rows == request
    remaining = len_ref[request] - seq_index * clen_dev
    scale = LOG2E / math.sqrt(HD)

    def scored(keys):
        return (
            lax.dot_general(
                keys, q_ref[...], (((1,), (1,)), ((), ())), preferred_element_type=jnp.float32
            )
            * scale
        )

    def weighted(weights, values):
        return lax.dot_general(
            weights.astype(jnp.bfloat16),
            values,
            (((0,), (0,)), ((), ())),
            preferred_element_type=jnp.float32,
        )

    def emit(out, top, total):
        high = total.astype(jnp.bfloat16).astype(jnp.float32)
        row = lax.broadcasted_iota(jnp.int32, (STAT_ROWS, rows), 0)
        stats = jnp.where(
            row == 0, top, jnp.where(row == 1, high, jnp.where(row == 2, total - high, 0.0))
        ).astype(jnp.bfloat16)
        for part in range(quarters):
            window = slice(part * tok_dev, (part + 1) * tok_dev)
            out_ref[part, :tok_dev, :] = out[window].astype(jnp.bfloat16)
            out_ref[part, tok_dev:, :] = stats[:, window]

    def rounded(top):
        return top.astype(jnp.bfloat16).astype(jnp.float32)

    floor = 0.1 * negative
    hidden = jnp.where(
        lax.broadcasted_iota(jnp.int32, (clen_dev, 1), 0) < remaining, 0.0, negative
    )

    @pl.when(own)
    def _():
        cached = scored(k_ref[0]) + hidden
        place = lax.broadcasted_iota(jnp.int32, (tok_dev, rows), 0) + own_start % rows
        seen = place <= lax.broadcasted_iota(jnp.int32, (tok_dev, rows), 1)
        fresh = jnp.where(seen, scored(nk_ref[...]), negative)
        top = jnp.maximum(jnp.max(cached, 0, keepdims=True), jnp.max(fresh, 0, keepdims=True))
        top = rounded(jnp.maximum(top, floor))
        cached = jnp.exp2(cached - top)
        fresh = jnp.exp2(fresh - top)
        total = jnp.sum(cached, 0, keepdims=True) + jnp.sum(fresh, 0, keepdims=True)
        emit(weighted(cached, v_ref[0]) + weighted(fresh, nv_ref[...]), top, total)

    @pl.when(jnp.logical_not(own) & (remaining > 0))
    def _():
        cached = scored(k_ref[0]) + hidden
        top = rounded(jnp.max(cached, 0, keepdims=True))
        cached = jnp.exp2(cached - top)
        emit(weighted(cached, v_ref[0]), top, jnp.sum(cached, 0, keepdims=True))

    @pl.when(jnp.logical_not(own) & (remaining <= 0))
    def _():
        emit(
            jnp.zeros((rows, HD), jnp.float32),
            jnp.full((1, rows), negative, jnp.float32),
            jnp.zeros((1, rows), jnp.float32),
        )


def attention(first, heads, lengths, every_query, cache_keys, cache_values, new_keys, new_values):
    requests, clen_dev, width = cache_keys.shape
    tok_dev = new_keys.shape[0]
    tokens = every_query.shape[0]
    quarters = NEW // tok_dev
    return pl.pallas_call(
        lambda *refs: attention_kernel(tok_dev, *refs),
        grid_spec=pltpu.PrefetchScalarGridSpec(
            num_scalar_prefetch=1,
            grid=(requests, heads),
            in_specs=[
                pl.BlockSpec((NEW, HD), lambda r, h, n: (r, first + h)),
                pl.BlockSpec((1, clen_dev, HD), lambda r, h, n: (r, 0, first + h)),
                pl.BlockSpec((1, clen_dev, HD), lambda r, h, n: (r, 0, first + h)),
                pl.BlockSpec((tok_dev, HD), lambda r, h, n: (0, first + h)),
                pl.BlockSpec((tok_dev, HD), lambda r, h, n: (0, first + h)),
            ],
            out_specs=pl.BlockSpec(
                (quarters, tok_dev + STAT_ROWS, HD), lambda r, h, n: (r, 0, h)
            ),
        ),
        out_shape=jax.ShapeDtypeStruct(
            (tokens // tok_dev, tok_dev + STAT_ROWS, heads * HD), jnp.bfloat16
        ),
        compiler_params=pltpu.CompilerParams(vmem_limit_bytes=56 * 1024 * 1024),
        cost_estimate=pl.CostEstimate(
            flops=4 * requests * NEW * clen_dev * heads * HD * 4,
            bytes_accessed=16 * 1024 * 1024,
            transcendentals=2 * NEW * clen_dev * heads,
        ),
        name="ragged_attention",
    )(lengths, every_query, cache_keys, cache_values, new_keys, new_values)


def gather_kernel(
    own_ref, out_ref, local_sem, zs, zr, xs, xr, ys, yr, fs, fr, gs, gr
):
    rows = own_ref.shape[0]
    half = rows // 2
    planes = lax.axis_size("seq") // 4
    me = lax.axis_index("seq")
    plane, corner = me // 4, me % 4
    side_x = corner + 1 - 2 * (corner % 2)
    side_y = (corner + 2) % 4
    step_by = jnp.where(plane < planes // 2, 1, planes - 1)

    def plane_at(k):
        return (plane + k * step_by) % planes

    def rows_of(index, start=0, size=rows):
        return pl.ds(pl.multiple_of(index * rows + start, half), size)

    def copy(src, dst, send, recv, target):
        return pltpu.make_async_remote_copy(
            src_ref=src,
            dst_ref=dst,
            send_sem=send,
            recv_sem=recv,
            device_id={"seq": target},
            device_id_type=pl.DeviceIdType.MESH,
        )

    barrier = pltpu.get_barrier_semaphore()
    peers = [plane_at(k) * 4 + corner for k in range(1, planes)]
    peers += [plane * 4 + side_x, plane * 4 + side_y]
    for peer in peers:
        pl.semaphore_signal(
            barrier, inc=1, device_id={"seq": peer}, device_id_type=pl.DeviceIdType.MESH
        )
    pl.semaphore_wait(barrier, len(peers))

    mine = pltpu.make_async_copy(own_ref, out_ref.at[rows_of(me)], local_sem)
    mine.start()
    sends = []
    for k in range(1, planes):
        target = plane_at(k)
        send = copy(
            own_ref, out_ref.at[rows_of(me)], zs.at[k], zr.at[plane], target * 4 + corner
        )
        send.start()
        sends.append(send)

    def arrived(index, start, size, sem):
        place = out_ref.at[rows_of(index, start, size)]
        pltpu.make_async_copy(place, place, sem).wait()

    def forward(k):
        level = plane_at(k)
        from_y = level * 4 + side_y
        arrived(from_y, 0, rows, yr.at[k])
        place = out_ref.at[rows_of(from_y, 0, half)]
        send = copy(place, place, fs.at[k], fr.at[k], plane * 4 + side_x)
        send.start()
        sends.append(send)
        from_x = level * 4 + side_x
        arrived(from_x, 0, rows, xr.at[k])
        place = out_ref.at[rows_of(from_x, half, half)]
        send = copy(place, place, gs.at[k], gr.at[k], plane * 4 + side_y)
        send.start()
        sends.append(send)

    for k in range(planes):
        level = plane_at(k)
        index = level * 4 + corner
        if k > 0:
            arrived(index, 0, rows, zr.at[level])
        place = out_ref.at[rows_of(index)]
        source = own_ref if k == 0 else place
        for send in (
            copy(source, place, xs.at[k], xr.at[k], plane * 4 + side_x),
            copy(source, place, ys.at[k], yr.at[k], plane * 4 + side_y),
        ):
            send.start()
            sends.append(send)
        if k > 0:
            forward(k - 1)
    forward(planes - 1)
    diagonal = 3 - corner
    for k in range(planes):
        arrived(plane_at(k) * 4 + diagonal, 0, half, fr.at[k])
        arrived(plane_at(k) * 4 + diagonal, half, half, gr.at[k])
    for send in sends:
        send.wait_send()
    mine.wait()


def gather_rows(rows, count):
    planes = count // 4
    return pl.pallas_call(
        gather_kernel,
        in_specs=[pl.BlockSpec(memory_space=pl.ANY)],
        out_specs=pl.BlockSpec(memory_space=pl.ANY),
        out_shape=jax.ShapeDtypeStruct((rows.shape[0] * count, rows.shape[1]), rows.dtype),
        scratch_shapes=[pltpu.SemaphoreType.DMA] + [pltpu.SemaphoreType.DMA((planes,))] * 10,
        compiler_params=pltpu.CompilerParams(
            collective_id=0, has_side_effects=True, vmem_limit_bytes=56 * 1024 * 1024
        ),
        name="gather_rows",
    )(rows)


def combine_kernel(parts_ref, out_ref):
    sources = parts_ref.shape[0]
    tok_dev = out_ref.shape[0]
    stats = [
        parts_ref[source, tok_dev:, :].astype(jnp.float32) for source in range(sources)
    ]
    tops = jnp.concatenate([stat[0:1] for stat in stats], 0)
    sums = jnp.concatenate([stat[1:2] + stat[2:3] for stat in stats], 0)
    factors = jnp.exp2(tops - jnp.max(tops, 0, keepdims=True))
    factors = factors / jnp.sum(factors * sums, 0, keepdims=True)
    columns = factors.T
    total = jnp.zeros((tok_dev, HD), jnp.float32)
    for source in range(sources):
        total += columns[:, source : source + 1] * parts_ref[source, :tok_dev, :].astype(
            jnp.float32
        )
    out_ref[...] = total.astype(jnp.bfloat16)


def combine(parts):
    sources, rows, width = parts.shape
    tok_dev = rows - STAT_ROWS
    return pl.pallas_call(
        combine_kernel,
        grid=(width // HD,),
        in_specs=[pl.BlockSpec((sources, rows, HD), lambda h: (0, 0, h))],
        out_specs=pl.BlockSpec((tok_dev, HD), lambda h: (0, h)),
        out_shape=jax.ShapeDtypeStruct((tok_dev, width), jnp.bfloat16),
        compiler_params=pltpu.CompilerParams(vmem_limit_bytes=32 * 1024 * 1024),
        name="combine_blocks",
    )(parts)


def shards(
    residual,
    queries,
    new_keys,
    new_values,
    cache_keys,
    cache_values,
    cache_lengths,
    out_proj,
    norm_gain,
    router,
    expert_ids,
    expert_gate_up,
    expert_down,
    shared_gate_up,
    shared_down,
):
    seq_count = lax.axis_size("seq")
    tensor_count = lax.axis_size("tensor")
    tok_dev = queries.shape[0]
    width_local = residual.shape[1]
    experts = router.shape[1]
    exp_dev = expert_gate_up.shape[0]
    topk = expert_ids.shape[1]
    every_query = gather_rows(queries, seq_count)
    heads_local = queries.shape[1] // HD
    early = max(heads_local // 4, 1)
    projected = 0.0
    for first, heads_piece in ((0, early), (early, heads_local - early)):
        if heads_piece == 0:
            continue
        partials = attention(
            first,
            heads_piece,
            cache_lengths,
            every_query,
            cache_keys,
            cache_values,
            new_keys,
            new_values,
        )
        attended = combine(
            lax.all_to_all(partials, "seq", split_axis=0, concat_axis=0, tiled=True)
        )
        features = slice(first * HD, (first + heads_piece) * HD)
        projected += jnp.dot(
            attended, out_proj[features], preferred_element_type=jnp.float32
        )
    attn_out = lax.psum_scatter(
        projected.astype(jnp.bfloat16), "tensor", scatter_dimension=1, tiled=True
    ).astype(jnp.float32)
    stream = residual.astype(jnp.float32) + attn_out
    square_total = lax.psum(jnp.sum(stream * stream, 1), "tensor")
    inverse_rms = lax.rsqrt(square_total / D + epsilon)
    normed = (stream * inverse_rms[:, None] * norm_gain).astype(jnp.bfloat16)
    logits = lax.psum(
        jnp.dot(normed, router, preferred_element_type=jnp.float32).astype(jnp.bfloat16), "tensor"
    ).astype(jnp.float32)
    matches = expert_ids[:, :, None] == lax.iota(jnp.int32, experts)[None, None, :]
    selected = jnp.sum(jnp.where(matches, logits[:, None, :], 0.0), 2)
    sigmoids = jax.nn.sigmoid(selected)
    gates = sigmoids / jnp.sum(sigmoids, 1, keepdims=True)
    normed_full = lax.all_gather(normed, "tensor", axis=1, tiled=True)
    shared_pair = jnp.einsum(
        "td,dcf->tcf", normed_full, shared_gate_up, preferred_element_type=jnp.float32
    )
    shared_act = (jax.nn.silu(shared_pair[:, 0]) * shared_pair[:, 1]).astype(jnp.bfloat16)
    shared_term = jnp.dot(shared_act, shared_down, preferred_element_type=jnp.float32)
    shared_out = lax.psum_scatter(
        shared_term.astype(jnp.bfloat16), "tensor", scatter_dimension=1, tiled=True
    ).astype(jnp.float32)
    cap = tensor_count * (
        (4 * tok_dev * topk + 3 * experts * tensor_count - 1) // (3 * experts * tensor_count)
    )
    flat_ids = expert_ids.reshape(-1)
    marks = (flat_ids[:, None] == lax.iota(jnp.int32, experts)[None, :]).astype(jnp.int32)
    earlier = jnp.cumsum(marks, 0) - marks
    rank = jnp.sum(earlier * marks, 1)
    slot_index = flat_ids * cap + rank
    slots = (
        (slot_index // (exp_dev * cap)) * cap + slot_index % cap
    ).reshape(tok_dev, topk)
    member = (expert_ids % exp_dev).reshape(tok_dev, topk)
    mixture = 0.0
    places = [
        (slots[:, :, None] == lax.iota(jnp.int32, seq_count * cap)[None, None, :])
        & (member[:, :, None] == local)
        for local in range(exp_dev)
    ]

    def received(local, after):
        placement = jnp.any(places[local], 1).astype(jnp.bfloat16)
        outgoing = lax.dot_general(
            placement, normed, (((0,), (0,)), ((), ())), preferred_element_type=jnp.float32
        ).astype(jnp.bfloat16)
        if after is not None:
            outgoing, after = lax.optimization_barrier((outgoing, after))
        incoming = lax.all_to_all(
            outgoing.reshape(seq_count, cap, width_local),
            "seq",
            split_axis=0,
            concat_axis=0,
            tiled=True,
        ).reshape(seq_count * cap, width_local)
        return incoming, after

    pairs = []
    incoming, _ = received(0, None)
    for local in range(exp_dev):
        following = None
        if local + 1 < exp_dev:
            following, incoming = received(local + 1, incoming)
        routed_rows = lax.all_gather(incoming, "tensor", axis=1, tiled=True)
        expert_pair = jnp.einsum(
            "rd,djf->rjf",
            routed_rows,
            expert_gate_up[local],
            preferred_element_type=jnp.float32,
        )
        if following is not None:
            incoming, expert_pair = lax.optimization_barrier((following, expert_pair))
        pairs.append(expert_pair)
    for local in range(exp_dev):
        here, expert_pair = places[local], pairs[local]
        expert_act = (jax.nn.silu(expert_pair[:, 0]) * expert_pair[:, 1]).astype(jnp.bfloat16)
        expert_term = jnp.dot(
            expert_act, expert_down[local], preferred_element_type=jnp.float32
        )
        expert_total = lax.psum_scatter(
            expert_term.astype(jnp.bfloat16), "tensor", scatter_dimension=1, tiled=True
        )
        returned = lax.all_to_all(
            expert_total.reshape(seq_count, cap, width_local),
            "seq",
            split_axis=0,
            concat_axis=0,
            tiled=True,
        ).reshape(seq_count * cap, width_local)
        portions = jnp.sum(jnp.where(here, gates[:, :, None], 0.0), 1)
        high = portions.astype(jnp.bfloat16)
        low = (portions - high.astype(jnp.float32)).astype(jnp.bfloat16)
        mixture += jnp.dot(high, returned, preferred_element_type=jnp.float32) + jnp.dot(
            low, returned, preferred_element_type=jnp.float32
        )
    return (stream + shared_out + mixture).astype(jnp.bfloat16)


def solution(mesh):
    in_specs = (
        P("seq", "tensor"),
        P("seq", "tensor"),
        P("seq", "tensor"),
        P("seq", "tensor"),
        P(None, "seq", "tensor"),
        P(None, "seq", "tensor"),
        P(),
        P("tensor", None),
        P("tensor"),
        P("tensor", None),
        P("seq", None),
        P("seq", None, None, "tensor"),
        P("seq", "tensor", None),
        P(None, None, "tensor"),
        P("tensor", None),
    )
    out_specs = P("seq", "tensor")
    return jax.shard_map(shards, mesh=mesh, in_specs=in_specs, out_specs=out_specs, check_vma=False)
```
